512 devices in a mesh: depth: 64 (over y, z_hi, core), res: 8 (over z_lo, x).
Axes of the slice: x: 4, y: 8, z: 8 (z_hi: 4, z_lo: 2; z = z_hi * 2 + z_lo), core: 2. Of those that a mesh axis runs over, the one named last changes fastest.
Arguments:
- row_q: bfloat16 [128, 512, 768], P('depth', 'res'), may hold values from -22 to 22
- row_k: bfloat16 [128, 512, 768], P('depth', 'res'), may hold values from -5 to 5
- row_v: bfloat16 [128, 512, 768], P('depth', 'res'), may hold values from -5 to 5
- col_q: bfloat16 [128, 512, 768], P('depth', 'res'), may hold values from -200 to 200
- col_k: bfloat16 [128, 512, 768], P('depth', 'res'), may hold values from -5 to 5
- col_v: bfloat16 [128, 512, 768], P('depth', 'res'), may hold values from -5 to 5
- cotangent: bfloat16 [128, 512, 768], P('depth', 'res'), may hold values from -5 to 5
Outputs:
- update: bfloat16 [128, 512, 768], P('depth', 'res')
- grad_row_q: bfloat16 [128, 512, 768], P('depth', 'res')
- grad_row_k: bfloat16 [128, 512, 768], P('depth', 'res')
- grad_row_v: bfloat16 [128, 512, 768], P('depth', 'res')
- grad_col_q: bfloat16 [128, 512, 768], P('depth', 'res')
- grad_col_k: bfloat16 [128, 512, 768], P('depth', 'res')
- grad_col_v: bfloat16 [128, 512, 768], P('depth', 'res')
The draws below stay inside these ranges and needn't reach their ends.
All inputs are finite; a program needn't handle non-finite values.
Results may differ from the reference program's by a relative error of at most 0.007.
Values may be sent and summed in bfloat16 or wider, within the bound.
No kernel may reach another device: no remote copies, remote signals or barrier semaphores. Data moves between devices by JAX's collectives and lax.ppermute only.
A program may use at most 64 MiB of HBM per device.

```python
import math
import jax
import jax.numpy as jnp
from jax import lax

H = 12
DH = 64
D = 768
ROWS = 128
COLS = 512


def row_base(key):
    return jnp.clip(jax.random.normal(jax.random.fold_in(key, 100), (ROWS, COLS, D), jnp.float32), -5.0, 5.0)


def col_base(key):
    return jnp.clip(jax.random.normal(jax.random.fold_in(key, 101), (ROWS, COLS, D), jnp.float32), -5.0, 5.0)


def draw_row_k(key, part):
    base = row_base(key)
    return base.astype(jnp.bfloat16)


def draw_col_k(key, part):
    base = col_base(key)
    return base.astype(jnp.bfloat16)


def draw_row_q(key, part):
    key = jax.random.fold_in(key, 5)
    own = jnp.clip(jax.random.normal(key, (ROWS, COLS, D), jnp.float32), -5.0, 5.0)
    return own.astype(jnp.bfloat16)


def draw_col_q(key, part):
    key = jax.random.fold_in(key, 6)
    own = jnp.clip(jax.random.normal(key, (ROWS, COLS, D), jnp.float32), -5.0, 5.0)
    return own.astype(jnp.bfloat16)


def shard_levels(own_key, dims, split, low, top_value):
    factor_of, own = 1.0, jax.random.fold_in(own_key, 6)
    for dim, blocks in split:
        draws = jnp.exp(jax.random.uniform(jax.random.fold_in(own, dim), (blocks,), jnp.float32, low / len(split), top_value / len(split)))
        factor_of = factor_of * jnp.repeat(draws, dims[dim] // blocks).reshape([-1 if axis == dim else 1 for axis in range(len(dims))])
    return factor_of


def noise(stream_key, extent, scale, most, pieces=(), held_as=jnp.bfloat16):
    result = scale * jax.random.normal(stream_key, extent, jnp.float32)
    if pieces:
        result = result * shard_levels(stream_key, extent, pieces, -0.22, 0.18)
    return jnp.clip(result, -most, most).astype(held_as)


def setup_inputs(seed: int = 0) -> dict:
    key_list = jax.random.split(jax.random.key(seed), 8)
    return {
        "row_q": draw_row_q(jax.random.fold_in(key_list[7], 71), 0),
        "row_k": draw_row_k(jax.random.fold_in(key_list[7], 71), 0),
        "row_v": noise(key_list[2], (ROWS, COLS, D), 1.0, 5.0, ((0, 64), (1, 8))),
        "col_q": draw_col_q(jax.random.fold_in(key_list[7], 71), 0),
        "col_k": draw_col_k(jax.random.fold_in(key_list[7], 71), 0),
        "col_v": noise(key_list[5], (ROWS, COLS, D), 1.0, 5.0, ((0, 64), (1, 8))),
        "cotangent": noise(key_list[6], (ROWS, COLS, D), 1.0, 5.0, ((0, 64), (1, 8))),
    }


def heads_first(array):
    return array.reshape(array.shape[0], array.shape[1], H, DH).transpose(2, 0, 1, 3)

def heads_last(array):
    return array.transpose(1, 2, 0, 3).reshape(array.shape[1], array.shape[2], H * DH)

def row_head(inputs):
    query, keys, values, grads = [item.astype(jnp.float32) for item in inputs]
    rows = query.shape[0]
    scale = 1.0 / math.sqrt(DH) / math.sqrt(rows)
    logits = jnp.einsum('rid,rjd->ij', query, keys) * scale
    probs = jax.nn.softmax(logits, axis=-1)
    probs_b = probs.astype(jnp.bfloat16).astype(jnp.float32)
    output = jnp.einsum('ij,rjd->rid', probs_b, values)
    dprobs = jnp.einsum('rid,rjd->ij', grads, values)
    dlogits = (probs * (dprobs - lax.optimization_barrier(jnp.sum(probs * dprobs, axis=-1, keepdims=True))) * scale).astype(jnp.bfloat16).astype(jnp.float32)
    grad_q = jnp.einsum('ij,rjd->rid', dlogits, keys).astype(jnp.bfloat16)
    grad_k = jnp.einsum('ij,rid->rjd', dlogits, query).astype(jnp.bfloat16)
    grad_v = jnp.einsum('ij,rid->rjd', probs_b, grads).astype(jnp.bfloat16)
    return (output, grad_q, grad_k, grad_v)

def col_head(inputs):
    query, keys, values, grads = [item.astype(jnp.float32) for item in inputs]
    scale = 1.0 / math.sqrt(DH)
    logits = jnp.einsum('rcd,scd->crs', query, keys) * scale
    probs = jax.nn.softmax(logits, axis=-1)
    probs_b = probs.astype(jnp.bfloat16).astype(jnp.float32)
    output = jnp.einsum('crs,scd->rcd', probs_b, values).astype(jnp.bfloat16)
    dprobs = jnp.einsum('rcd,scd->crs', grads, values)
    dlogits = (probs * (dprobs - lax.optimization_barrier(jnp.sum(probs * dprobs, axis=-1, keepdims=True))) * scale).astype(jnp.bfloat16).astype(jnp.float32)
    grad_q = jnp.einsum('crs,scd->rcd', dlogits, keys).astype(jnp.bfloat16)
    grad_k = jnp.einsum('crs,rcd->scd', dlogits, query).astype(jnp.bfloat16)
    grad_v = jnp.einsum('crs,rcd->scd', probs_b, grads).astype(jnp.bfloat16)
    return (output, grad_q, grad_k, grad_v)

def reference(row_q, row_k, row_v, col_q, col_k, col_v, cotangent):
    grads_h = heads_first(cotangent)
    row_out, grq, grk, grv = lax.map(row_head, (heads_first(row_q), heads_first(row_k), heads_first(row_v), grads_h))
    col_out, gcq, gck, gcv = lax.map(col_head, (heads_first(col_q), heads_first(col_k), heads_first(col_v), grads_h))
    update = (heads_last(row_out) + heads_last(col_out).astype(jnp.float32)).astype(jnp.bfloat16)
    return (update, heads_last(grq), heads_last(grk), heads_last(grv), heads_last(gcq), heads_last(gck), heads_last(gcv))
```

```python
import math

import jax
import jax.numpy as jnp
from jax import lax
from jax.experimental import pallas as pl
from jax.experimental.pallas import tpu as pltpu
from jax.sharding import Mesh, PartitionSpec as P

H = 12
DH = 64
ROWS = 128
COLS = 512
HG = ("ylo", "core")
RED = ("yhi", "zhi")
DEP = ("yhi", "ylo", "zhi", "core")
RES = ("zlo", "x")
NHG = 4
HL = 3
NRED = 16
NRES = 8
CB = 64
QR = HL * CB // NRED
ROW_SCALE = 1.0 / math.sqrt(DH) / math.sqrt(ROWS)
COL_SCALE = 1.0 / math.sqrt(DH)
bf = jnp.bfloat16
f32 = jnp.float32


def call(body, out_shape, *args, flops=10**8):
    many = isinstance(out_shape, (list, tuple))
    outs = out_shape if many else [out_shape]
    nbytes = sum(math.prod(a.shape) * a.dtype.itemsize for a in list(args) + list(outs))
    return pl.pallas_call(
        body,
        out_shape=out_shape,
        in_specs=[pl.BlockSpec(memory_space=pltpu.VMEM)] * len(args),
        out_specs=[pl.BlockSpec(memory_space=pltpu.VMEM)] * len(outs)
        if many
        else pl.BlockSpec(memory_space=pltpu.VMEM),
        compiler_params=pltpu.CompilerParams(vmem_limit_bytes=40 * 2**20),
        cost_estimate=pl.CostEstimate(flops=flops, bytes_accessed=nbytes, transcendentals=0),
    )(*args)


def sds(shape, dtype):
    return jax.ShapeDtypeStruct(shape, dtype)


def dot(a, b, ca, cb):
    return lax.dot_general(a, b, (((ca,), (cb,)), ((), ())), preferred_element_type=f32)


def to_heads_kernel(*refs):
    out = refs[-1]
    for n, ref in enumerate(refs[:-1]):
        for h in range(H):
            a = ref[0, :, h * DH : (h + 1) * DH]
            b = ref[1, :, h * DH : (h + 1) * DH]
            out[h // HL, n, h % HL] = jnp.concatenate([a, b], axis=1)


def logits_kernel(mine, keys_values, out):
    for h in range(HL):
        parts = []
        for n, which in ((2, 0), (3, 1)):
            lhs = jnp.concatenate([mine[s, n, h] for s in range(NHG)], axis=1)
            rhs = jnp.concatenate(
                [
                    jnp.concatenate([keys_values[r, s, which, h] for r in range(NRES)], axis=0)
                    for s in range(NHG)
                ],
                axis=1,
            )
            parts.append(dot(lhs, rhs, 1, 1))
        for i in range(0, CB, 4):
            row = h * CB + i
            m, q = row // QR, row % QR
            out[m, q : q + 4, :] = parts[0][i : i + 4]
            out[m, QR + q : QR + q + 4, :] = parts[1][i : i + 4]


def softmax_kernel(parts, out):
    total = parts[0]
    for m in range(1, NRED):
        total = total + parts[m]
    logits = total[:QR] * ROW_SCALE
    dprobs = total[QR:]
    e = jnp.exp(logits - jnp.max(logits, axis=-1, keepdims=True))
    probs = e / jnp.sum(e, axis=-1, keepdims=True)
    dl = probs * (dprobs - jnp.sum(probs * dprobs, axis=-1, keepdims=True)) * ROW_SCALE
    both = jnp.concatenate([probs, dl], axis=0).astype(bf)
    for m in range(NRED):
        out[m] = both


def assemble_kernel(rows, probs, dlogits, by_key):
    parts = [rows[m].astype(f32) for m in range(NRED)]
    p = jnp.concatenate([a[:QR] for a in parts], axis=0).astype(bf)
    d = jnp.concatenate([a[QR:] for a in parts], axis=0).astype(bf)
    probs[...] = p
    dlogits[...] = d
    for r in range(NRES):
        by_key[r] = jnp.concatenate(
            [p[:, r * CB : (r + 1) * CB], d[:, r * CB : (r + 1) * CB]], axis=1
        )


def query_side_kernel(probs, dlogits, keys_values, out):
    for h in range(HL):
        for n, (lhs, which) in enumerate(((probs, 1), (dlogits, 0))):
            rhs = jnp.concatenate(
                [
                    jnp.concatenate([keys_values[r, s, which, h] for s in range(NHG)], axis=1)
                    for r in range(NRES)
                ],
                axis=0,
            )
            res = dot(lhs[h * CB : (h + 1) * CB, :], rhs, 1, 0).astype(bf)
            for s in range(NHG):
                out[s, n, h] = res[:, s * 2 * DH : (s + 1) * 2 * DH]


def key_side_kernel(by_query, queries, grads, out):
    for h in range(HL):
        lhs = jnp.concatenate(
            [by_query[r, h * CB : (h + 1) * CB, :] for r in range(NRES)], axis=0
        )
        for n, (ref, low) in enumerate(((queries, CB), (grads, 0))):
            rhs = jnp.concatenate(
                [
                    jnp.concatenate([ref[r, s, h] for s in range(NHG)], axis=1)
                    for r in range(NRES)
                ],
                axis=0,
            )
            res = dot(lhs, rhs, 0, 0)[low : low + CB].astype(bf)
            for s in range(NHG):
                out[s, n, h] = res[:, s * 2 * DH : (s + 1) * 2 * DH]


def column_kernel(query, keys, values, grads, out):
    lane = lax.broadcasted_iota(jnp.int32, (ROWS, 2 * DH), 1)
    first = lane < DH
    zero = jnp.zeros((ROWS, 2 * DH), bf)
    for pair in range(H // 2):
        at = slice(pair * 2 * DH, (pair + 1) * 2 * DH)
        q, k, v, g = (ref[:, at] for ref in (query, keys, values, grads))
        res = []
        for half in range(2):
            keep = first if half == 0 else jnp.logical_not(first)
            logits = dot(jnp.where(keep, q, zero), k, 1, 1) * COL_SCALE
            dprobs = dot(jnp.where(keep, g, zero), v, 1, 1)
            e = jnp.exp(logits - jnp.max(logits, axis=-1, keepdims=True))
            probs = e / jnp.sum(e, axis=-1, keepdims=True)
            dl = probs * (dprobs - jnp.sum(probs * dprobs, axis=-1, keepdims=True)) * COL_SCALE
            pb = probs.astype(bf)
            db = dl.astype(bf)
            res.append((dot(pb, v, 1, 0), dot(db, k, 1, 0), dot(db, q, 0, 0), dot(pb, g, 0, 0)))
        for n in range(4):
            out[n, :, at] = jnp.where(first, res[0][n], res[1][n]).astype(bf)


def finish_kernel(rows, col_out, update, grad_q, grad_k, grad_v):
    for pair in range(H // 2):
        for n, ref in enumerate((update, grad_q, grad_k, grad_v)):
            a, b = (rows[h // HL, n, h % HL] for h in (2 * pair, 2 * pair + 1))
            for r in range(2):
                got = jnp.concatenate(
                    [a[:, r * DH : (r + 1) * DH], b[:, r * DH : (r + 1) * DH]], axis=1
                )
                at = slice(pair * 2 * DH, (pair + 1) * 2 * DH)
                if n == 0:
                    got = (got.astype(f32) + col_out[r, :, at].astype(f32)).astype(bf)
                ref[r, :, at] = got


def swap(array, axes):
    return lax.all_to_all(array, axes, 0, 0, tiled=True)


def on_device(row_q, row_k, row_v, col_q, col_k, col_v, cotangent):
    dev = sds((2, CB, H * DH), bf)
    by_head = call(
        to_heads_kernel, sds((NHG, 4, HL, CB, 2 * DH), bf), row_k, row_v, row_q, cotangent
    )
    mine = swap(by_head, HG)
    queries = lax.all_gather(mine[:, 2], RES, axis=0)
    grads = lax.all_gather(mine[:, 3], RES, axis=0)
    own_kv = mine[:, :2]
    keys_values = swap(jnp.broadcast_to(own_kv, (NRES,) + own_kv.shape), RES)

    cols = jnp.stack([col_q, col_k, col_v, cotangent]).transpose(2, 0, 1, 3)
    cols = swap(cols.reshape(CB, 8, H * DH), DEP)
    cols = cols.reshape(CB, 4, 2, H * DH).transpose(1, 0, 2, 3).reshape(4, ROWS, H * DH)

    parts = call(logits_kernel, sds((NRED, 2 * QR, COLS), f32), mine, keys_values)
    parts = swap(parts, RED)
    rows = call(softmax_kernel, sds((NRED, 2 * QR, COLS), bf), parts)
    rows = swap(rows, RED)
    probs, dlogits, by_key = call(
        assemble_kernel,
        [
            sds((HL * CB, COLS), bf),
            sds((HL * CB, COLS), bf),
            sds((NRES, HL * CB, 2 * CB), bf),
        ],
        rows,
    )
    by_query = swap(by_key, RES)
    side = sds((NHG, 2, HL, CB, 2 * DH), bf)
    query_side = call(query_side_kernel, side, probs, dlogits, keys_values)

    done = call(column_kernel, sds((4, ROWS, H * DH), bf), cols[0], cols[1], cols[2], cols[3])
    done = done.reshape(4, CB, 2, H * DH).transpose(1, 0, 2, 3).reshape(CB, 8, H * DH)
    done = swap(done, DEP)
    done = done.reshape(CB, 4, 2, H * DH).transpose(1, 2, 0, 3)

    key_side = call(key_side_kernel, side, by_query, queries, grads)
    back = swap(jnp.concatenate([query_side, key_side], axis=1), HG)
    update, grad_rq, grad_rk, grad_rv = call(finish_kernel, [dev] * 4, back, done[0])
    return update, grad_rq, grad_rk, grad_rv, done[1], done[2], done[3]


def solution(mesh):
    fine = Mesh(
        mesh.devices.reshape(4, 2, 4, 2, 2, 4), ("yhi", "ylo", "zhi", "core", "zlo", "x")
    )
    spec = P(DEP, RES, None)
    return jax.shard_map(
        on_device, mesh=fine, in_specs=(spec,) * 7, out_specs=(spec,) * 7, check_vma=False
    )
```

```python
import math

import jax
import jax.numpy as jnp
from jax import lax
from jax.experimental import pallas as pl
from jax.experimental.pallas import tpu as pltpu
from jax.sharding import Mesh, PartitionSpec as P

H = 12
DH = 64
ROWS = 128
COLS = 512
HG = ("ylo", "core")
RED = ("yhi", "zhi")
DEP = ("yhi", "ylo", "zhi", "core")
RES = ("zlo", "x")
NHG = 4
HL = 3
NRED = 16
NRES = 8
CB = 64
QR = HL * CB // NRED
ROW_SCALE = 1.0 / math.sqrt(DH) / math.sqrt(ROWS)
COL_SCALE = 1.0 / math.sqrt(DH)
bf = jnp.bfloat16
f32 = jnp.float32


def call(body, out_shape, *args, scratch=(), alias=None, inside=True, flops=10**7):
    many = isinstance(out_shape, (list, tuple))
    outs = out_shape if many else [out_shape]
    nbytes = sum(math.prod(a.shape) * a.dtype.itemsize for a in list(args) + list(outs))
    spec = pl.BlockSpec(memory_space=pltpu.VMEM) if inside else pl.BlockSpec()
    return pl.pallas_call(
        body,
        out_shape=out_shape,
        in_specs=[spec] * len(args),
        out_specs=[spec] * len(outs) if many else spec,
        scratch_shapes=list(scratch),
        input_output_aliases=alias or {},
        compiler_params=pltpu.CompilerParams(vmem_limit_bytes=40 * 2**20),
        cost_estimate=pl.CostEstimate(flops=flops, bytes_accessed=nbytes, transcendentals=0),
    )(*args)


def sds(shape, dtype):
    return jax.ShapeDtypeStruct(shape, dtype)


def dot(a, b, ca, cb):
    return lax.dot_general(a, b, (((ca,), (cb,)), ((), ())), preferred_element_type=f32)


def to_heads_kernel(*refs):
    out = refs[-1]
    for n, ref in enumerate(refs[:-1]):
        for h in range(H):
            a = ref[0, :, h * DH : (h + 1) * DH]
            b = ref[1, :, h * DH : (h + 1) * DH]
            out[h // HL, n, h % HL] = jnp.concatenate([a, b], axis=1)


def logits_kernel(mine, keys_values, out):
    for h in range(HL):
        parts = []
        for n, which in ((2, 0), (3, 1)):
            lhs = jnp.concatenate([mine[s, n, h] for s in range(NHG)], axis=1)
            rhs = jnp.concatenate(
                [
                    jnp.concatenate([keys_values[r, s, which, h] for r in range(NRES)], axis=0)
                    for s in range(NHG)
                ],
                axis=1,
            )
            parts.append(dot(lhs, rhs, 1, 1))
        for i in range(0, CB, 4):
            row = h * CB + i
            m, q = row // QR, row % QR
            out[m, q : q + 4, :] = parts[0][i : i + 4]
            out[m, QR + q : QR + q + 4, :] = parts[1][i : i + 4]


def softmax_kernel(parts, out):
    total = parts[0]
    for m in range(1, NRED):
        total = total + parts[m]
    logits = total[:QR] * ROW_SCALE
    dprobs = total[QR:]
    e = jnp.exp(logits - jnp.max(logits, axis=-1, keepdims=True))
    probs = e / jnp.sum(e, axis=-1, keepdims=True)
    dl = probs * (dprobs - jnp.sum(probs * dprobs, axis=-1, keepdims=True)) * ROW_SCALE
    both = jnp.concatenate([probs, dl], axis=0).astype(bf)
    for m in range(NRED):
        out[m] = both


def assemble_kernel(rows, probs, dlogits, by_key):
    parts = [rows[m].astype(f32) for m in range(NRED)]
    p = jnp.concatenate([a[:QR] for a in parts], axis=0).astype(bf)
    d = jnp.concatenate([a[QR:] for a in parts], axis=0).astype(bf)
    probs[...] = p
    dlogits[...] = d
    for r in range(NRES):
        by_key[r] = jnp.concatenate(
            [p[:, r * CB : (r + 1) * CB], d[:, r * CB : (r + 1) * CB]], axis=1
        )


def query_side_kernel(probs, dlogits, keys_values, out):
    for h in range(HL):
        for n, (lhs, which) in enumerate(((probs, 1), (dlogits, 0))):
            rhs = jnp.concatenate(
                [
                    jnp.concatenate([keys_values[r, s, which, h] for s in range(NHG)], axis=1)
                    for r in range(NRES)
                ],
                axis=0,
            )
            res = dot(lhs[h * CB : (h + 1) * CB, :], rhs, 1, 0).astype(bf)
            for s in range(NHG):
                out[s, n, h] = res[:, s * 2 * DH : (s + 1) * 2 * DH]


def key_side_kernel(by_query, queries_grads, half, out):
    del half
    for h in range(HL):
        lhs = jnp.concatenate(
            [by_query[r, h * CB : (h + 1) * CB, :] for r in range(NRES)], axis=0
        )
        for n, low in ((0, CB), (1, 0)):
            rhs = jnp.concatenate(
                [
                    jnp.concatenate([queries_grads[r, s, n, h] for s in range(NHG)], axis=1)
                    for r in range(NRES)
                ],
                axis=0,
            )
            res = dot(lhs, rhs, 0, 0)[low : low + CB].astype(bf)
            for s in range(NHG):
                out[s, 2 + n, h] = res[:, s * 2 * DH : (s + 1) * 2 * DH]


def by_column_kernel(query, keys, values, grads, out, rows):
    for pair in range(H // 2):
        at = slice(pair * 2 * DH, (pair + 1) * 2 * DH)
        for n, ref in enumerate((query, keys, values, grads)):
            for r in range(2):
                rows[pair, pl.ds(2 * n + r, CB, stride=8), :] = ref[r, :, at].astype(f32)
        out[:, at] = rows[pair].astype(bf)


def column_kernel(got, out, rows):
    lane = lax.broadcasted_iota(jnp.int32, (ROWS, 2 * DH), 1)
    first = lane < DH
    zero = jnp.zeros((ROWS, 2 * DH), bf)
    for pair in range(H // 2):
        at = slice(pair * 2 * DH, (pair + 1) * 2 * DH)
        rows[pair] = got[:, at].astype(f32)
        q, k, v, g = (
            jnp.concatenate(
                [rows[pair, pl.ds(2 * n + r, CB, stride=8), :] for r in range(2)], axis=0
            ).astype(bf)
            for n in range(4)
        )
        res = []
        for half in range(2):
            keep = first if half == 0 else jnp.logical_not(first)
            logits = dot(jnp.where(keep, q, zero), k, 1, 1) * COL_SCALE
            dprobs = dot(jnp.where(keep, g, zero), v, 1, 1)
            e = jnp.exp(logits - jnp.max(logits, axis=-1, keepdims=True))
            probs = e / jnp.sum(e, axis=-1, keepdims=True)
            dl = probs * (dprobs - jnp.sum(probs * dprobs, axis=-1, keepdims=True)) * COL_SCALE
            pb = probs.astype(bf)
            db = dl.astype(bf)
            res.append((dot(pb, v, 1, 0), dot(db, k, 1, 0), dot(db, q, 0, 0), dot(pb, g, 0, 0)))
        for n in range(4):
            both = jnp.where(first, res[0][n], res[1][n])
            for r in range(2):
                rows[pair, pl.ds(2 * n + r, CB, stride=8), :] = both[r * CB : (r + 1) * CB]
        out[:, at] = rows[pair].astype(bf)


def column_finish_kernel(columns, col_out, grad_cq, grad_ck, grad_cv, rows):
    for pair in range(H // 2):
        at = slice(pair * 2 * DH, (pair + 1) * 2 * DH)
        rows[pair] = columns[:, at].astype(f32)
        for n, ref in enumerate((col_out, grad_cq, grad_ck, grad_cv)):
            for r in range(2):
                ref[r, :, at] = rows[pair, pl.ds(2 * n + r, CB, stride=8), :].astype(bf)


def finish_kernel(heads, col_out, update, grad_rq, grad_rk, grad_rv):
    for pair in range(H // 2):
        at = slice(pair * 2 * DH, (pair + 1) * 2 * DH)
        for n, ref in enumerate((update, grad_rq, grad_rk, grad_rv)):
            a, b = (heads[h // HL, n, h % HL] for h in (2 * pair, 2 * pair + 1))
            for r in range(2):
                got = jnp.concatenate(
                    [a[:, r * DH : (r + 1) * DH], b[:, r * DH : (r + 1) * DH]], axis=1
                )
                if n == 0:
                    got = (got.astype(f32) + col_out[r, :, at].astype(f32)).astype(bf)
                ref[r, :, at] = got


def swap(array, axes):
    return lax.all_to_all(array, axes, 0, 0, tiled=True)


def on_device(row_q, row_k, row_v, col_q, col_k, col_v, cotangent):
    dev = sds((2, CB, H * DH), bf)
    flat = sds((CB * 8, H * DH), bf)
    room = pltpu.VMEM((H // 2, CB * 8, 2 * DH), f32)
    by_head = call(
        to_heads_kernel,
        sds((NHG, 4, HL, CB, 2 * DH), bf),
        row_k,
        row_v,
        row_q,
        cotangent,
        inside=False,
    )
    mine = swap(by_head, HG)
    keys_values = lax.all_gather(mine[:, :2], RES, axis=0)
    queries_grads = lax.all_gather(mine[:, 2:], RES, axis=0)

    cols = call(
        by_column_kernel, flat, col_q, col_k, col_v, cotangent, scratch=[room], inside=False
    )
    cols, mine = lax.optimization_barrier((cols, mine))
    cols = swap(cols, DEP)
    cols = call(column_kernel, flat, cols, scratch=[room], flops=10**9)
    cols = swap(cols, DEP)
    cols, mine = lax.optimization_barrier((cols, mine))

    parts = call(logits_kernel, sds((NRED, 2 * QR, COLS), f32), mine, keys_values)
    parts = swap(parts, RED)
    rows = call(softmax_kernel, sds((NRED, 2 * QR, COLS), bf), parts)
    rows = swap(rows, RED)
    col_out, grad_cq, grad_ck, grad_cv = call(
        column_finish_kernel, [dev] * 4, cols, scratch=[room], inside=False
    )
    probs, dlogits, by_key = call(
        assemble_kernel,
        [
            sds((HL * CB, COLS), bf),
            sds((HL * CB, COLS), bf),
            sds((NRES, HL * CB, 2 * CB), bf),
        ],
        rows,
    )
    by_query = swap(by_key, RES)
    back = sds((NHG, 4, HL, CB, 2 * DH), bf)
    half = call(query_side_kernel, back, probs, dlogits, keys_values)
    back = call(key_side_kernel, back, by_query, queries_grads, half, alias={2: 0})
    back = swap(back, HG)
    update, grad_rq, grad_rk, grad_rv = call(
        finish_kernel, [dev] * 4, back, col_out, inside=False
    )
    return update, grad_rq, grad_rk, grad_rv, grad_cq, grad_ck, grad_cv


def solution(mesh):
    fine = Mesh(
        mesh.devices.reshape(4, 2, 4, 2, 2, 4), ("yhi", "ylo", "zhi", "core", "zlo", "x")
    )
    spec = P(DEP, RES, None)
    return jax.shard_map(
        on_device, mesh=fine, in_specs=(spec,) * 7, out_specs=(spec,) * 7, check_vma=False
    )
```

```python
import math

import jax
import jax.numpy as jnp
from jax import lax
from jax.experimental import pallas as pl
from jax.experimental.pallas import tpu as pltpu
from jax.sharding import Mesh, PartitionSpec as P

H = 12
DH = 64
ROWS = 128
COLS = 512
HG = ("ylo", "core")
HGZ = ("ylo", "core", "zlo")
RED = ("yhi", "zhi")
DEP = ("yhi", "ylo", "zhi", "core")
RES = ("zlo", "x")
NHG = 4
HL = 3
NRED = 16
NRES = 8
NX = 4
NZ = 2
CB = 64
QR = HL * CB // NRED
ROW_SCALE = 1.0 / math.sqrt(DH) / math.sqrt(ROWS)
COL_SCALE = 1.0 / math.sqrt(DH)
bf = jnp.bfloat16
f32 = jnp.float32


def call(body, out_shape, *args, scratch=(), inside=True, flops=10**7):
    many = isinstance(out_shape, (list, tuple))
    outs = out_shape if many else [out_shape]
    nbytes = sum(math.prod(a.shape) * a.dtype.itemsize for a in list(args) + list(outs))
    spec = pl.BlockSpec(memory_space=pltpu.VMEM) if inside else pl.BlockSpec()
    return pl.pallas_call(
        body,
        out_shape=out_shape,
        in_specs=[spec] * len(args),
        out_specs=[spec] * len(outs) if many else spec,
        scratch_shapes=list(scratch),
        compiler_params=pltpu.CompilerParams(vmem_limit_bytes=(24 if inside else 56) * 2**20),
        cost_estimate=pl.CostEstimate(flops=flops, bytes_accessed=nbytes, transcendentals=0),
    )(*args)


def sds(shape, dtype):
    return jax.ShapeDtypeStruct(shape, dtype)


def dot(a, b, ca, cb):
    return lax.dot_general(a, b, (((ca,), (cb,)), ((), ())), preferred_element_type=f32)


def to_heads_kernel(*refs):
    out = refs[-1]
    for n, ref in enumerate(refs[:-1]):
        for h in range(H):
            a = ref[0, :, h * DH : (h + 1) * DH]
            b = ref[1, :, h * DH : (h + 1) * DH]
            both = jnp.concatenate([a, b], axis=1)
            for z in range(NZ):
                out[h // HL, z, n, h % HL] = both


def gathered(ref, n, h):
    return jnp.concatenate(
        [
            jnp.concatenate([ref[x, s, z, n, h] for s in range(NHG)], axis=1)
            for z in range(NZ)
            for x in range(NX)
        ],
        axis=0,
    )


def logits_kernel(mine, keys_values, out):
    own = lax.axis_index("zlo")
    logits, dprobs = [], []
    for h in range(HL):
        for res, n, which in ((logits, 0, 0), (dprobs, 1, 1)):
            lhs = jnp.concatenate([mine[s, own, n, h] for s in range(NHG)], axis=1)
            res.append(dot(lhs, gathered(keys_values, which, h), 1, 1))
    logits = jnp.concatenate(logits, axis=0)
    dprobs = jnp.concatenate(dprobs, axis=0)
    dprobs = dprobs - jnp.mean(dprobs, axis=-1, keepdims=True)
    high = logits.astype(bf).astype(f32)
    rest = logits - high
    for m in range(NRED):
        at = slice(m * QR, (m + 1) * QR)
        out[m] = jnp.concatenate([high[at], rest[at], dprobs[at]], axis=0).astype(bf)


def softmax_kernel(parts, out):
    total = parts[0].astype(f32)
    for m in range(1, NRED):
        total = total + parts[m].astype(f32)
    logits = (total[:QR] + total[QR : 2 * QR]) * ROW_SCALE
    dprobs = total[2 * QR :]
    e = jnp.exp(logits - jnp.max(logits, axis=-1, keepdims=True))
    probs = e / jnp.sum(e, axis=-1, keepdims=True)
    dl = probs * (dprobs - jnp.sum(probs * dprobs, axis=-1, keepdims=True)) * ROW_SCALE
    both = jnp.concatenate([probs, dl], axis=0).astype(bf)
    for m in range(NRED):
        out[m] = both


def assemble_kernel(rows, probs, dlogits, by_key):
    parts = [rows[m].astype(f32) for m in range(NRED)]
    p = jnp.concatenate([a[:QR] for a in parts], axis=0).astype(bf)
    d = jnp.concatenate([a[QR:] for a in parts], axis=0).astype(bf)
    probs[...] = p
    dlogits[...] = d
    for r in range(NRES):
        by_key[r] = jnp.concatenate(
            [p[:, r * CB : (r + 1) * CB], d[:, r * CB : (r + 1) * CB]], axis=1
        )


def row_grads_kernel(probs, dlogits, by_query, keys_values, queries_grads, out):

    def put(n, h, res):
        for s in range(NHG):
            out[s, n, h] = res[:, s * 2 * DH : (s + 1) * 2 * DH].astype(bf)

    for h in range(HL):
        at = slice(h * CB, (h + 1) * CB)
        put(0, h, dot(probs[at, :], gathered(keys_values, 1, h), 1, 0))
        put(1, h, dot(dlogits[at, :], gathered(keys_values, 0, h), 1, 0))
        lhs = jnp.concatenate([by_query[r, at, :] for r in range(NRES)], axis=0)
        put(2, h, dot(lhs, gathered(queries_grads, 0, h), 0, 0)[CB:])
        put(3, h, dot(lhs, gathered(queries_grads, 1, h), 0, 0)[:CB])


def by_column_kernel(query, keys, values, grads, out, rows):
    for pair in range(H // 2):
        at = slice(pair * 2 * DH, (pair + 1) * 2 * DH)
        for n, ref in enumerate((query, keys, values, grads)):
            for r in range(2):
                rows[pair, pl.ds(2 * n + r, CB, stride=8), :] = ref[r, :, at].astype(f32)
        out[:, at] = rows[pair].astype(bf)


def column_kernel(got, out, rows):
    low = lax.broadcasted_iota(jnp.int32, (ROWS, 2 * DH), 1) < DH
    zero = jnp.zeros((ROWS, 2 * DH), bf)

    def stacked(x):
        return jnp.concatenate([jnp.where(low, x, zero), jnp.where(low, zero, x)], axis=0)

    def beside(x):
        return jnp.concatenate([x[:ROWS], x[ROWS:]], axis=1)

    for pair in range(H // 2):
        at = slice(pair * 2 * DH, (pair + 1) * 2 * DH)
        rows[pair] = got[:, at].astype(f32)
        q, k, v, g = (
            jnp.concatenate(
                [rows[pair, pl.ds(2 * n + r, CB, stride=8), :] for r in range(2)], axis=0
            ).astype(bf)
            for n in range(4)
        )
        qs, ks, vs, gs = (stacked(x) for x in (q, k, v, g))
        logits = dot(qs, k, 1, 1) * COL_SCALE
        dprobs = dot(gs, v, 1, 1)
        e = jnp.exp(logits - jnp.max(logits, axis=-1, keepdims=True))
        probs = e / jnp.sum(e, axis=-1, keepdims=True)
        dl = probs * (dprobs - jnp.sum(probs * dprobs, axis=-1, keepdims=True)) * COL_SCALE
        pb = probs.astype(bf)
        db = dl.astype(bf)
        res = (
            dot(beside(pb), vs, 1, 0),
            dot(beside(db), ks, 1, 0),
            dot(db, qs, 0, 0),
            dot(pb, gs, 0, 0),
        )
        for n in range(4):
            for r in range(2):
                rows[pair, pl.ds(2 * n + r, CB, stride=8), :] = res[n][r * CB : (r + 1) * CB]
        out[:, at] = rows[pair].astype(bf)


def column_finish_kernel(columns, col_out, grad_cq, grad_ck, grad_cv, rows):
    for pair in range(H // 2):
        at = slice(pair * 2 * DH, (pair + 1) * 2 * DH)
        rows[pair] = columns[:, at].astype(f32)
        for n, ref in enumerate((col_out, grad_cq, grad_ck, grad_cv)):
            for r in range(2):
                ref[r, :, at] = rows[pair, pl.ds(2 * n + r, CB, stride=8), :].astype(bf)


def finish_kernel(heads, col_out, update, grad_rq, grad_rk, grad_rv):
    for pair in range(H // 2):
        at = slice(pair * 2 * DH, (pair + 1) * 2 * DH)
        for n, ref in enumerate((update, grad_rq, grad_rk, grad_rv)):
            a, b = (heads[h // HL, n, h % HL] for h in (2 * pair, 2 * pair + 1))
            for r in range(2):
                got = jnp.concatenate(
                    [a[:, r * DH : (r + 1) * DH], b[:, r * DH : (r + 1) * DH]], axis=1
                )
                if n == 0:
                    got = (got.astype(f32) + col_out[r, :, at].astype(f32)).astype(bf)
                ref[r, :, at] = got


def swap(array, axes):
    return lax.all_to_all(array, axes, 0, 0, tiled=True)


def on_device(row_q, row_k, row_v, col_q, col_k, col_v, cotangent):
    dev = sds((2, CB, H * DH), bf)
    flat = sds((CB * 8, H * DH), bf)
    room = pltpu.VMEM((H // 2, CB * 8, 2 * DH), f32)
    by_head = call(
        to_heads_kernel,
        sds((NHG, NZ, 4, HL, CB, 2 * DH), bf),
        row_k,
        row_v,
        row_q,
        cotangent,
        inside=False,
    )
    mine = swap(by_head.reshape((NHG * NZ,) + by_head.shape[2:]), HGZ).reshape(by_head.shape)
    keys_values, mine = mine[:, :, :2], mine[:, :, 2:]
    keys_values = lax.all_gather(keys_values, "x", axis=0)
    queries_grads = lax.all_gather(mine, "x", axis=0)

    cols = call(
        by_column_kernel, flat, col_q, col_k, col_v, cotangent, scratch=[room]
    )
    cols, mine = lax.optimization_barrier((cols, mine))
    cols = swap(cols, DEP)
    cols = call(column_kernel, flat, cols, scratch=[room], flops=10**9)
    cols = swap(cols, DEP)
    cols, mine = lax.optimization_barrier((cols, mine))

    parts = call(
        logits_kernel,
        sds((NRED, 3 * QR, COLS), bf),
        mine,
        keys_values,
    )
    parts = swap(parts, RED)
    rows = call(softmax_kernel, sds((NRED, 2 * QR, COLS), bf), parts)
    rows = swap(rows, RED)
    col_out, grad_cq, grad_ck, grad_cv = call(
        column_finish_kernel, [dev] * 4, cols, scratch=[room], inside=False
    )
    rows, queries_grads, col_out = lax.optimization_barrier((rows, queries_grads, col_out))
    probs, dlogits, by_key = call(
        assemble_kernel,
        [
            sds((HL * CB, COLS), bf),
            sds((HL * CB, COLS), bf),
            sds((NRES, HL * CB, 2 * CB), bf),
        ],
        rows,
    )
    by_query = swap(by_key, RES)
    back = call(
        row_grads_kernel,
        sds((NHG, 4, HL, CB, 2 * DH), bf),
        probs,
        dlogits,
        by_query,
        keys_values,
        queries_grads,
    )
    back = swap(back, HG)
    update, grad_rq, grad_rk, grad_rv = call(
        finish_kernel, [dev] * 4, back, col_out, inside=False
    )
    return update, grad_rq, grad_rk, grad_rv, grad_cq, grad_ck, grad_cv


def solution(mesh):
    fine = Mesh(
        mesh.devices.reshape(4, 2, 4, 2, 2, 4), ("yhi", "ylo", "zhi", "core", "zlo", "x")
    )
    spec = P(DEP, RES, None)
    return jax.shard_map(
        on_device, mesh=fine, in_specs=(spec,) * 7, out_specs=(spec,) * 7, check_vma=False
    )
```

```python
import math

import jax
import jax.numpy as jnp
from jax import lax
from jax.experimental import pallas as pl
from jax.experimental.pallas import tpu as pltpu
from jax.sharding import Mesh, PartitionSpec as P

H = 12
DH = 64
ROWS = 128
COLS = 512
HG = ("ylo", "core")
HGZ = ("ylo", "core", "zlo")
RED = ("yhi", "zhi")
DEP = ("yhi", "ylo", "zhi", "core")
RES = ("zlo", "x")
NHG = 4
HL = 3
NRED = 16
NRES = 8
NX = 4
NZ = 2
CB = 64
QR = HL * CB // NRED
ROW_SCALE = 1.0 / math.sqrt(DH) / math.sqrt(ROWS)
COL_SCALE = 1.0 / math.sqrt(DH)
HALVES = (slice(0, COLS // 2), slice(COLS // 2, COLS))
bf = jnp.bfloat16
f32 = jnp.float32


def call(body, out_shape, *args, scratch=(), inside=True, out_inside=None, flops=10**7):
    many = isinstance(out_shape, (list, tuple))
    outs = out_shape if many else [out_shape]
    nbytes = sum(math.prod(a.shape) * a.dtype.itemsize for a in list(args) + list(outs))
    spec, out_spec = (
        pl.BlockSpec(memory_space=pltpu.VMEM) if place else pl.BlockSpec()
        for place in (inside, inside if out_inside is None else out_inside)
    )
    return pl.pallas_call(
        body,
        out_shape=out_shape,
        in_specs=[spec] * len(args),
        out_specs=[out_spec] * len(outs) if many else out_spec,
        scratch_shapes=list(scratch),
        compiler_params=pltpu.CompilerParams(vmem_limit_bytes=(24 if inside else 56) * 2**20),
        cost_estimate=pl.CostEstimate(flops=flops, bytes_accessed=nbytes, transcendentals=0),
    )(*args)


def sds(shape, dtype):
    return jax.ShapeDtypeStruct(shape, dtype)


def dot(a, b, ca, cb):
    return lax.dot_general(a, b, (((ca,), (cb,)), ((), ())), preferred_element_type=f32)


def to_heads_kernel(*refs):
    out = refs[-1]
    for n, ref in enumerate(refs[:-1]):
        for h in range(H):
            a = ref[0, :, h * DH : (h + 1) * DH]
            b = ref[1, :, h * DH : (h + 1) * DH]
            both = jnp.concatenate([a, b], axis=1)
            for z in range(NZ):
                out[h // HL, z, n, h % HL] = both


def gathered(ref, n, h):
    return jnp.concatenate(
        [
            jnp.concatenate([ref[x, s, z, n, h] for s in range(NHG)], axis=1)
            for z in range(NZ)
            for x in range(NX)
        ],
        axis=0,
    )


def logits_kernel(mine, keys_values, out):
    own = lax.axis_index("zlo")
    logits, dprobs = [], []
    for h in range(HL):
        for res, n, which in ((logits, 0, 0), (dprobs, 1, 1)):
            lhs = jnp.concatenate([mine[s, own, n, h] for s in range(NHG)], axis=1)
            res.append(dot(lhs, gathered(keys_values, which, h), 1, 1))
    logits = jnp.concatenate(logits, axis=0)
    dprobs = jnp.concatenate(dprobs, axis=0)
    dprobs = dprobs - jnp.mean(dprobs, axis=-1, keepdims=True)
    high = logits.astype(bf).astype(f32)
    rest = logits - high
    for m in range(NRED):
        at = slice(m * QR, (m + 1) * QR)
        out[m] = jnp.concatenate(
            [a[at, half] for a in (high, rest, dprobs) for half in HALVES], axis=0
        ).astype(bf)


def softmax_kernel(parts, out):
    total = parts[0].astype(f32)
    for m in range(1, NRED):
        total = total + parts[m].astype(f32)
    high, rest, dprobs = (
        jnp.concatenate([total[n * QR : (n + 1) * QR], total[(n + 1) * QR : (n + 2) * QR]], axis=1)
        for n in (0, 2, 4)
    )
    logits = (high + rest) * ROW_SCALE
    e = jnp.exp(logits - jnp.max(logits, axis=-1, keepdims=True))
    probs = e / jnp.sum(e, axis=-1, keepdims=True)
    dl = probs * (dprobs - jnp.sum(probs * dprobs, axis=-1, keepdims=True)) * ROW_SCALE
    both = jnp.concatenate([probs, dl], axis=0).astype(bf)
    for m in range(NRED):
        out[m] = both


def assemble_kernel(rows, probs, dlogits, by_key):
    parts = [rows[m].astype(f32) for m in range(NRED)]
    p = jnp.concatenate([a[:QR] for a in parts], axis=0).astype(bf)
    d = jnp.concatenate([a[QR:] for a in parts], axis=0).astype(bf)
    probs[...] = p
    dlogits[...] = d
    for r in range(NRES):
        by_key[r] = jnp.concatenate(
            [p[:, r * CB : (r + 1) * CB], d[:, r * CB : (r + 1) * CB]], axis=1
        )


def row_grads_kernel(probs, dlogits, by_query, keys_values, queries_grads, out):

    def put(n, h, res):
        for s in range(NHG):
            out[s, n, h] = res[:, s * 2 * DH : (s + 1) * 2 * DH].astype(bf)

    for h in range(HL):
        at = slice(h * CB, (h + 1) * CB)
        put(0, h, dot(probs[at, :], gathered(keys_values, 1, h), 1, 0))
        put(1, h, dot(dlogits[at, :], gathered(keys_values, 0, h), 1, 0))
        lhs = jnp.concatenate([by_query[r, at, :] for r in range(NRES)], axis=0)
        put(2, h, dot(lhs, gathered(queries_grads, 0, h), 0, 0)[CB:])
        put(3, h, dot(lhs, gathered(queries_grads, 1, h), 0, 0)[:CB])


def by_column_kernel(query, keys, values, grads, out, rows):
    for pair in range(H // 2):
        at = slice(pair * 2 * DH, (pair + 1) * 2 * DH)
        for n, ref in enumerate((query, keys, values, grads)):
            for r in range(2):
                rows[pair, pl.ds(2 * n + r, CB, stride=8), :] = ref[r, :, at].astype(f32)
        out[:, at] = rows[pair].astype(bf)


def column_kernel(got, out, rows):
    low = lax.broadcasted_iota(jnp.int32, (ROWS, 2 * DH), 1) < DH
    zero = jnp.zeros((ROWS, 2 * DH), bf)

    def stacked(x):
        return jnp.concatenate([jnp.where(low, x, zero), jnp.where(low, zero, x)], axis=0)

    def beside(x):
        return jnp.concatenate([x[:ROWS], x[ROWS:]], axis=1)

    for pair in range(H // 2):
        at = slice(pair * 2 * DH, (pair + 1) * 2 * DH)
        rows[pair] = got[:, at].astype(f32)
        q, k, v, g = (
            jnp.concatenate(
                [rows[pair, pl.ds(2 * n + r, CB, stride=8), :] for r in range(2)], axis=0
            ).astype(bf)
            for n in range(4)
        )
        qs, ks, vs, gs = (stacked(x) for x in (q, k, v, g))
        logits = dot(qs, k, 1, 1) * COL_SCALE
        dprobs = dot(gs, v, 1, 1)
        e = jnp.exp(logits - jnp.max(logits, axis=-1, keepdims=True))
        probs = e / jnp.sum(e, axis=-1, keepdims=True)
        dl = probs * (dprobs - jnp.sum(probs * dprobs, axis=-1, keepdims=True)) * COL_SCALE
        pb = probs.astype(bf)
        db = dl.astype(bf)
        res = (
            dot(beside(pb), vs, 1, 0),
            dot(beside(db), ks, 1, 0),
            dot(db, qs, 0, 0),
            dot(pb, gs, 0, 0),
        )
        for n in range(4):
            for r in range(2):
                rows[pair, pl.ds(2 * n + r, CB, stride=8), :] = res[n][r * CB : (r + 1) * CB]
        out[:, at] = rows[pair].astype(bf)


def column_finish_kernel(columns, col_out, grad_cq, grad_ck, grad_cv, rows):
    for pair in range(H // 2):
        at = slice(pair * 2 * DH, (pair + 1) * 2 * DH)
        rows[pair] = columns[:, at].astype(f32)
        for n, ref in enumerate((col_out, grad_cq, grad_ck, grad_cv)):
            for r in range(2):
                ref[r, :, at] = rows[pair, pl.ds(2 * n + r, CB, stride=8), :].astype(bf)


def finish_kernel(heads, col_out, update, grad_rq, grad_rk, grad_rv):
    for pair in range(H // 2):
        at = slice(pair * 2 * DH, (pair + 1) * 2 * DH)
        for n, ref in enumerate((update, grad_rq, grad_rk, grad_rv)):
            a, b = (heads[h // HL, n, h % HL] for h in (2 * pair, 2 * pair + 1))
            for r in range(2):
                got = jnp.concatenate(
                    [a[:, r * DH : (r + 1) * DH], b[:, r * DH : (r + 1) * DH]], axis=1
                )
                if n == 0:
                    got = (got.astype(f32) + col_out[r, :, at].astype(f32)).astype(bf)
                ref[r, :, at] = got


def swap(array, axes):
    return lax.all_to_all(array, axes, 0, 0, tiled=True)


def on_device(row_q, row_k, row_v, col_q, col_k, col_v, cotangent):
    dev = sds((2, CB, H * DH), bf)
    flat = sds((CB * 8, H * DH), bf)
    room = pltpu.VMEM((H // 2, CB * 8, 2 * DH), f32)
    by_head = call(
        to_heads_kernel,
        sds((NHG, NZ, 4, HL, CB, 2 * DH), bf),
        row_k,
        row_v,
        row_q,
        cotangent,
        inside=False,
    )
    mine = swap(by_head.reshape((NHG * NZ,) + by_head.shape[2:]), HGZ).reshape(by_head.shape)
    cols = call(by_column_kernel, flat, col_q, col_k, col_v, cotangent, scratch=[room])
    cols, mine = lax.optimization_barrier((cols, mine))
    keys_values, mine = mine[:, :, :2], mine[:, :, 2:]
    keys_values = lax.all_gather(keys_values, "x", axis=0)
    queries_grads = lax.all_gather(mine, "x", axis=0)

    cols = swap(cols, DEP)
    cols = call(column_kernel, flat, cols, scratch=[room], flops=10**9)
    cols = swap(cols, DEP)

    parts = call(
        logits_kernel,
        sds((NRED, 6 * QR, COLS // 2), bf),
        mine,
        keys_values,
    )
    cols, parts = lax.optimization_barrier((cols, parts))
    parts = swap(parts, RED)
    rows = call(softmax_kernel, sds((NRED, 2 * QR, COLS), bf), parts)
    rows = swap(rows, RED)
    col_out, grad_cq, grad_ck, grad_cv = call(
        column_finish_kernel, [dev] * 4, cols, scratch=[room], inside=False
    )
    rows, queries_grads, col_out = lax.optimization_barrier((rows, queries_grads, col_out))
    probs, dlogits, by_key = call(
        assemble_kernel,
        [
            sds((HL * CB, COLS), bf),
            sds((HL * CB, COLS), bf),
            sds((NRES, HL * CB, 2 * CB), bf),
        ],
        rows,
    )
    by_query = swap(by_key, RES)
    back = call(
        row_grads_kernel,
        sds((NHG, 4, HL, CB, 2 * DH), bf),
        probs,
        dlogits,
        by_query,
        keys_values,
        queries_grads,
    )
    back = swap(back, HG)
    update, grad_rq, grad_rk, grad_rv = call(
        finish_kernel, [dev] * 4, back, col_out, out_inside=False
    )
    return update, grad_rq, grad_rk, grad_rv, grad_cq, grad_ck, grad_cv


def solution(mesh):
    fine = Mesh(
        mesh.devices.reshape(4, 2, 4, 2, 2, 4), ("yhi", "ylo", "zhi", "core", "zlo", "x")
    )
    spec = P(DEP, RES, None)
    return jax.shard_map(
        on_device, mesh=fine, in_specs=(spec,) * 7, out_specs=(spec,) * 7, check_vma=False
    )
```

```python
import math

import jax
import jax.numpy as jnp
from jax import lax
from jax.experimental import pallas as pl
from jax.experimental.pallas import tpu as pltpu
from jax.sharding import Mesh, PartitionSpec as P

H = 12
DH = 64
ROWS = 128
COLS = 512
NEAR = ("ylo", "zlo", "core")
RED = ("yhi", "zhi")
DEP = ("yhi", "ylo", "zhi", "core")
RES = ("zlo", "x")
BLOCKS = ("core", "x")
NHG = 4
SEQS = ((0, 0), (0, 1), (1, 0), (1, 1))
HL = 3
NRED = 16
NRES = 8
NX = 4
NZ = 2
NC = 2
HC = 32
CB = 64
QR = HL * CB // NRED
ROW_SCALE = 1.0 / math.sqrt(DH) / math.sqrt(ROWS)
COL_SCALE = 1.0 / math.sqrt(DH)
HALVES = (slice(0, COLS // 2), slice(COLS // 2, COLS))
bf = jnp.bfloat16
f32 = jnp.float32


def call(body, out_shape, *args, scratch=(), inside=True, out_inside=None, flops=10**7):
    many = isinstance(out_shape, (list, tuple))
    outs = out_shape if many else [out_shape]
    nbytes = sum(math.prod(a.shape) * a.dtype.itemsize for a in list(args) + list(outs))
    specs = {
        True: pl.BlockSpec(memory_space=pltpu.VMEM),
        False: pl.BlockSpec(),
        "far": pl.BlockSpec(memory_space=pl.ANY),
    }
    spec, out_spec = specs[inside], specs[inside if out_inside is None else out_inside]
    return pl.pallas_call(
        body,
        out_shape=out_shape,
        in_specs=[spec] * len(args),
        out_specs=[out_spec] * len(outs) if many else out_spec,
        scratch_shapes=list(scratch),
        compiler_params=pltpu.CompilerParams(vmem_limit_bytes=(24 if inside is True else 56) * 2**20),
        cost_estimate=pl.CostEstimate(flops=flops, bytes_accessed=nbytes, transcendentals=0),
    )(*args)


def sds(shape, dtype):
    return jax.ShapeDtypeStruct(shape, dtype)


def dot(a, b, ca, cb):
    return lax.dot_general(a, b, (((ca,), (cb,)), ((), ())), preferred_element_type=f32)


def to_heads_kernel(*refs):
    arrays, (out, got, made, in_sems, out_sems) = refs[:4], refs[4:]
    reads = [
        pltpu.make_async_copy(ref, got.at[n], in_sems.at[n]) for n, ref in enumerate(arrays)
    ]
    for copy in reads:
        copy.start()
    writes = []
    for n, read in enumerate(reads):
        read.wait()
        for h in range(H):
            a = got[n, 0, :, h * DH : (h + 1) * DH]
            b = got[n, 1, :, h * DH : (h + 1) * DH]
            both = jnp.concatenate([a, b], axis=1)
            for c in range(NC):
                made[n, h // HL * NC + c, h % HL] = both[c * HC : (c + 1) * HC]
        writes.append(pltpu.make_async_copy(made.at[n], out.at[:, n], out_sems.at[n]))
        writes[-1].start()
    for copy in writes:
        copy.wait()


def block(ref, at, n, h):
    return jnp.concatenate(
        [
            jnp.concatenate([ref[(*at, (y * NZ + z) * NC + c, n, h)] for y, c in SEQS], axis=1)
            for z in range(NZ)
        ],
        axis=0,
    )


def gathered(ref, n, h):
    return jnp.concatenate(
        [block(ref, (x, c), n, h) for c in range(NC) for x in range(NX)], axis=0
    )


def logits_kernel(mine, keys_values, out):
    logits, dprobs = [], []
    for h in range(HL):
        for res, n, which in ((logits, 0, 0), (dprobs, 1, 1)):
            res.append(dot(block(mine, (), n, h), gathered(keys_values, which, h), 1, 1))
    logits = jnp.concatenate(logits, axis=0)
    dprobs = jnp.concatenate(dprobs, axis=0)
    dprobs = dprobs - jnp.mean(dprobs, axis=-1, keepdims=True)
    high = logits.astype(bf).astype(f32)
    rest = logits - high
    for m in range(NRED):
        at = slice(m * QR, (m + 1) * QR)
        out[m] = jnp.concatenate(
            [a[at, half] for a in (high, rest, dprobs) for half in HALVES], axis=0
        ).astype(bf)


def softmax_kernel(parts, out):
    total = parts[0].astype(f32)
    for m in range(1, NRED):
        total = total + parts[m].astype(f32)
    high, rest, dprobs = (
        jnp.concatenate([total[n * QR : (n + 1) * QR], total[(n + 1) * QR : (n + 2) * QR]], axis=1)
        for n in (0, 2, 4)
    )
    logits = (high + rest) * ROW_SCALE
    e = jnp.exp(logits - jnp.max(logits, axis=-1, keepdims=True))
    probs = e / jnp.sum(e, axis=-1, keepdims=True)
    dl = probs * (dprobs - jnp.sum(probs * dprobs, axis=-1, keepdims=True)) * ROW_SCALE
    both = jnp.concatenate([probs, dl], axis=0).astype(bf)
    for m in range(NRED):
        out[m] = both


def assemble_kernel(rows, probs, dlogits, by_key):
    parts = [rows[m].astype(f32) for m in range(NRED)]
    p = jnp.concatenate([a[:QR] for a in parts], axis=0).astype(bf)
    d = jnp.concatenate([a[QR:] for a in parts], axis=0).astype(bf)
    probs[...] = p
    dlogits[...] = d
    for r in range(NRES):
        by_key[r] = jnp.concatenate(
            [p[:, r * CB : (r + 1) * CB], d[:, r * CB : (r + 1) * CB]], axis=1
        )


def row_grads_kernel(probs, dlogits, by_query, keys_values, queries_grads, out):

    def put(n, h, res):
        for z in range(NZ):
            for s, (y, c) in enumerate(SEQS):
                out[(y * NZ + z) * NC + c, n, h] = res[
                    z * HC : (z + 1) * HC, s * 2 * DH : (s + 1) * 2 * DH
                ].astype(bf)

    for h in range(HL):
        at = slice(h * CB, (h + 1) * CB)
        put(0, h, dot(probs[at, :], gathered(keys_values, 1, h), 1, 0))
        put(1, h, dot(dlogits[at, :], gathered(keys_values, 0, h), 1, 0))
        lhs = jnp.concatenate([by_query[r, at, :] for r in range(NRES)], axis=0)
        put(2, h, dot(lhs, gathered(queries_grads, 0, h), 0, 0)[CB:])
        put(3, h, dot(lhs, gathered(queries_grads, 1, h), 0, 0)[:CB])


def by_column_kernel(query, keys, values, grads, out, rows):
    for pair in range(H // 2):
        at = slice(pair * 2 * DH, (pair + 1) * 2 * DH)
        for n, ref in enumerate((query, keys, values, grads)):
            for r in range(2):
                rows[pair, pl.ds(2 * n + r, CB, stride=8), :] = ref[r, :, at].astype(f32)
        out[:, at] = rows[pair].astype(bf)


def column_kernel(got, out, rows, made, sems):
    low = lax.broadcasted_iota(jnp.int32, (ROWS, 2 * DH), 1) < DH
    zero = jnp.zeros((ROWS, 2 * DH), bf)

    def stacked(x):
        return jnp.concatenate([jnp.where(low, x, zero), jnp.where(low, zero, x)], axis=0)

    def beside(x):
        return jnp.concatenate([x[:ROWS], x[ROWS:]], axis=1)

    copies = []
    for pair in range(H // 2):
        at = slice(pair * 2 * DH, (pair + 1) * 2 * DH)
        rows[pair] = got[:, at].astype(f32)
        q, k, v, g = (
            jnp.concatenate(
                [rows[pair, pl.ds(2 * n + r, CB, stride=8), :] for r in range(2)], axis=0
            ).astype(bf)
            for n in range(4)
        )
        qs, ks, vs, gs = (stacked(x) for x in (q, k, v, g))
        logits = dot(qs, k, 1, 1) * COL_SCALE
        dprobs = dot(gs, v, 1, 1)
        e = jnp.exp(logits - jnp.max(logits, axis=-1, keepdims=True))
        probs = e / jnp.sum(e, axis=-1, keepdims=True)
        dl = probs * (dprobs - jnp.sum(probs * dprobs, axis=-1, keepdims=True)) * COL_SCALE
        pb = probs.astype(bf)
        db = dl.astype(bf)
        res = (
            dot(beside(pb), vs, 1, 0),
            dot(beside(db), ks, 1, 0),
            dot(db, qs, 0, 0),
            dot(pb, gs, 0, 0),
        )
        for n in range(4):
            for r in range(2):
                rows[pair, pl.ds(2 * n + r, CB, stride=8), :] = res[n][r * CB : (r + 1) * CB]
        made[pair] = rows[pair].astype(bf)
        copies.append(pltpu.make_async_copy(made.at[pair], out.at[:, at], sems.at[pair]))
        copies[-1].start()
    for copy in copies:
        copy.wait()


def column_finish_kernel(columns, col_out, grad_cq, grad_ck, grad_cv, rows):
    for pair in range(H // 2):
        at = slice(pair * 2 * DH, (pair + 1) * 2 * DH)
        rows[pair] = columns[:, at].astype(f32)
        for n, ref in enumerate((col_out, grad_cq, grad_ck, grad_cv)):
            for r in range(2):
                ref[r, :, at] = rows[pair, pl.ds(2 * n + r, CB, stride=8), :].astype(bf)


def finish_kernel(heads, col_out, update, grad_rq, grad_rk, grad_rv):
    for pair in range(H // 2):
        at = slice(pair * 2 * DH, (pair + 1) * 2 * DH)
        for n, ref in enumerate((update, grad_rq, grad_rk, grad_rv)):
            a, b = (
                jnp.concatenate([heads[h // HL * NC + c, n, h % HL] for c in range(NC)], axis=0)
                for h in (2 * pair, 2 * pair + 1)
            )
            for r in range(2):
                got = jnp.concatenate(
                    [a[:, r * DH : (r + 1) * DH], b[:, r * DH : (r + 1) * DH]], axis=1
                )
                if n == 0:
                    got = (got.astype(f32) + col_out[r, :, at].astype(f32)).astype(bf)
                ref[r, :, at] = got


def swap(array, axes):
    return lax.all_to_all(array, axes, 0, 0, tiled=True)


def on_device(row_q, row_k, row_v, col_q, col_k, col_v, cotangent):
    dev = sds((2, CB, H * DH), bf)
    flat = sds((CB * 8, H * DH), bf)
    room = pltpu.VMEM((H // 2, CB * 8, 2 * DH), f32)
    by_head = call(
        to_heads_kernel,
        sds((NHG * NC, 4, HL, HC, 2 * DH), bf),
        row_k,
        row_v,
        row_q,
        cotangent,
        scratch=[
            pltpu.VMEM((4, 2, CB, H * DH), bf),
            pltpu.VMEM((4, NHG * NC, HL, HC, 2 * DH), bf),
            pltpu.SemaphoreType.DMA((4,)),
            pltpu.SemaphoreType.DMA((4,)),
        ],
        inside="far",
    )
    mine = swap(by_head, NEAR)
    cols = call(by_column_kernel, flat, col_q, col_k, col_v, cotangent, scratch=[room])
    cols, mine = lax.optimization_barrier((cols, mine))
    first = lax.axis_index("core") == 0
    other = lax.ppermute(mine, "core", [(0, 1), (1, 0)])

    def spread(n):
        own, far = mine[:, n : n + 2], other[:, n : n + 2]
        both = jnp.stack([jnp.where(first, own, far), jnp.where(first, far, own)])
        return lax.all_gather(both, "x", axis=0)

    keys_values = spread(0)
    queries_grads = spread(2)
    mine = mine[:, 2:]

    cols = swap(cols, DEP)
    cols = call(
        column_kernel,
        flat,
        cols,
        scratch=[
            room,
            pltpu.VMEM((H // 2, CB * 8, 2 * DH), bf),
            pltpu.SemaphoreType.DMA((H // 2,)),
        ],
        out_inside="far",
        flops=10**9,
    )
    cols = swap(cols, DEP)

    parts = call(
        logits_kernel,
        sds((NRED, 6 * QR, COLS // 2), bf),
        mine,
        keys_values,
    )
    cols, parts = lax.optimization_barrier((cols, parts))
    parts = swap(parts, RED)
    rows = call(softmax_kernel, sds((NRED, 2 * QR, COLS), bf), parts)
    rows = swap(rows, RED)
    col_out, grad_cq, grad_ck, grad_cv = call(
        column_finish_kernel, [dev] * 4, cols, scratch=[room], inside=False
    )
    rows, queries_grads, col_out = lax.optimization_barrier((rows, queries_grads, col_out))
    probs, dlogits, by_key = call(
        assemble_kernel,
        [
            sds((HL * CB, COLS), bf),
            sds((HL * CB, COLS), bf),
            sds((NRES, HL * CB, 2 * CB), bf),
        ],
        rows,
    )
    by_query = swap(by_key, BLOCKS)
    back = call(
        row_grads_kernel,
        sds((NHG * NC, 4, HL, HC, 2 * DH), bf),
        probs,
        dlogits,
        by_query,
        keys_values,
        queries_grads,
    )
    back = swap(back, NEAR)
    update, grad_rq, grad_rk, grad_rv = call(
        finish_kernel, [dev] * 4, back, col_out, out_inside=False
    )
    return update, grad_rq, grad_rk, grad_rv, grad_cq, grad_ck, grad_cv


def solution(mesh):
    fine = Mesh(
        mesh.devices.reshape(4, 2, 4, 2, 2, 4), ("yhi", "ylo", "zhi", "core", "zlo", "x")
    )
    spec = P(DEP, RES, None)
    return jax.shard_map(
        on_device, mesh=fine, in_specs=(spec,) * 7, out_specs=(spec,) * 7, check_vma=False
    )
```

```python
import math

import jax
import jax.numpy as jnp
from jax import lax
from jax.experimental import pallas as pl
from jax.experimental.pallas import tpu as pltpu
from jax.sharding import Mesh, PartitionSpec as P

H = 12
DH = 64
ROWS = 128
COLS = 512
NEAR = ("ylo", "zlo", "core")
RED = ("zhi", "yhi")
DEP = ("yhi", "ylo", "zhi", "core")
COLUMN = ("zhi", "yhi", "ylo", "core")
RES = ("zlo", "x")
BLOCKS = ("core", "x")
NHG = 4
SEQS = ((0, 0), (0, 1), (1, 0), (1, 1))
HL = 3
NRED = 16
NRES = 8
NX = 4
NZ = 2
NC = 2
HC = 32
CB = 64
QR = HL * CB // NRED
ROW_SCALE = 1.0 / math.sqrt(DH) / math.sqrt(ROWS)
COL_SCALE = 1.0 / math.sqrt(DH)
HALVES = (slice(0, COLS // 2), slice(COLS // 2, COLS))
bf = jnp.bfloat16
f32 = jnp.float32


def call(body, out_shape, *args, scratch=(), inside=True, out_inside=None, flops=10**7):
    many = isinstance(out_shape, (list, tuple))
    outs = out_shape if many else [out_shape]
    nbytes = sum(math.prod(a.shape) * a.dtype.itemsize for a in list(args) + list(outs))
    specs = {
        True: pl.BlockSpec(memory_space=pltpu.VMEM),
        False: pl.BlockSpec(),
        "far": pl.BlockSpec(memory_space=pl.ANY),
    }
    spec, out_spec = specs[inside], specs[inside if out_inside is None else out_inside]
    return pl.pallas_call(
        body,
        out_shape=out_shape,
        in_specs=[spec] * len(args),
        out_specs=[out_spec] * len(outs) if many else out_spec,
        scratch_shapes=list(scratch),
        compiler_params=pltpu.CompilerParams(vmem_limit_bytes=(24 if inside is True else 56) * 2**20),
        cost_estimate=pl.CostEstimate(flops=flops, bytes_accessed=nbytes, transcendentals=0),
    )(*args)


def sds(shape, dtype):
    return jax.ShapeDtypeStruct(shape, dtype)


def dot(a, b, ca, cb):
    return lax.dot_general(a, b, (((ca,), (cb,)), ((), ())), preferred_element_type=f32)


def to_heads_kernel(*refs):
    arrays, (out, got, made, in_sems, out_sems) = refs[:4], refs[4:]
    reads = [
        pltpu.make_async_copy(ref, got.at[n], in_sems.at[n]) for n, ref in enumerate(arrays)
    ]
    for copy in reads:
        copy.start()
    writes = []
    for n, read in enumerate(reads):
        read.wait()
        for h in range(H):
            a = got[n, 0, :, h * DH : (h + 1) * DH]
            b = got[n, 1, :, h * DH : (h + 1) * DH]
            both = jnp.concatenate([a, b], axis=1)
            for c in range(NC):
                made[n, h // HL * NC + c, h % HL] = both[c * HC : (c + 1) * HC]
        writes.append(pltpu.make_async_copy(made.at[n], out.at[:, n], out_sems.at[n]))
        writes[-1].start()
    for copy in writes:
        copy.wait()


def block(ref, at, n, h):
    return jnp.concatenate(
        [
            jnp.concatenate([ref[(*at, (y * NZ + z) * NC + c, n, h)] for y, c in SEQS], axis=1)
            for z in range(NZ)
        ],
        axis=0,
    )


def gathered(ref, n, h):
    return jnp.concatenate(
        [block(ref, (x, c), n, h) for c in range(NC) for x in range(NX)], axis=0
    )


def logits_kernel(mine, keys_values, out):
    logits, dprobs = [], []
    for h in range(HL):
        for res, n, which in ((logits, 0, 0), (dprobs, 1, 1)):
            res.append(dot(block(mine, (), n, h), gathered(keys_values, which, h), 1, 1))
    logits = jnp.concatenate(logits, axis=0)
    dprobs = jnp.concatenate(dprobs, axis=0)
    dprobs = dprobs - jnp.mean(dprobs, axis=-1, keepdims=True)
    high = logits.astype(bf).astype(f32)
    rest = logits - high
    for m in range(NRED):
        at = slice(m * QR, (m + 1) * QR)
        out[m] = jnp.concatenate(
            [a[at, half] for a in (high, rest, dprobs) for half in HALVES], axis=0
        ).astype(bf)


def softmax_kernel(parts, out):
    total = parts[0].astype(f32)
    for m in range(1, NRED):
        total = total + parts[m].astype(f32)
    high, rest, dprobs = (
        jnp.concatenate([total[n * QR : (n + 1) * QR], total[(n + 1) * QR : (n + 2) * QR]], axis=1)
        for n in (0, 2, 4)
    )
    logits = (high + rest) * ROW_SCALE
    e = jnp.exp(logits - jnp.max(logits, axis=-1, keepdims=True))
    probs = e / jnp.sum(e, axis=-1, keepdims=True)
    dl = probs * (dprobs - jnp.sum(probs * dprobs, axis=-1, keepdims=True)) * ROW_SCALE
    both = jnp.concatenate([probs, dl], axis=0).astype(bf)
    for m in range(NRED):
        out[m] = both


def assemble_kernel(rows, probs, dlogits, by_key):
    parts = [rows[m].astype(f32) for m in range(NRED)]
    p = jnp.concatenate([a[:QR] for a in parts], axis=0).astype(bf)
    d = jnp.concatenate([a[QR:] for a in parts], axis=0).astype(bf)
    probs[...] = p
    dlogits[...] = d
    for r in range(NRES):
        by_key[r] = jnp.concatenate(
            [p[:, r * CB : (r + 1) * CB], d[:, r * CB : (r + 1) * CB]], axis=1
        )


def row_grads_kernel(probs, dlogits, by_query, keys_values, queries_grads, out):

    def put(n, h, res):
        for z in range(NZ):
            for s, (y, c) in enumerate(SEQS):
                out[(y * NZ + z) * NC + c, n, h] = res[
                    z * HC : (z + 1) * HC, s * 2 * DH : (s + 1) * 2 * DH
                ].astype(bf)

    for h in range(HL):
        at = slice(h * CB, (h + 1) * CB)
        put(0, h, dot(probs[at, :], gathered(keys_values, 1, h), 1, 0))
        put(1, h, dot(dlogits[at, :], gathered(keys_values, 0, h), 1, 0))
        lhs = jnp.concatenate([by_query[r, at, :] for r in range(NRES)], axis=0)
        put(2, h, dot(lhs, gathered(queries_grads, 0, h), 0, 0)[CB:])
        put(3, h, dot(lhs, gathered(queries_grads, 1, h), 0, 0)[:CB])


def by_column_kernel(query, keys, values, grads, out, rows):
    for pair in range(H // 2):
        at = slice(pair * 2 * DH, (pair + 1) * 2 * DH)
        for n, ref in enumerate((query, keys, values, grads)):
            for r in range(2):
                rows[pair, pl.ds(2 * n + r, CB, stride=8), :] = ref[r, :, at].astype(f32)
        out[:, at] = rows[pair].astype(bf)


def column_kernel(got, out, rows, made, sems):
    low = lax.broadcasted_iota(jnp.int32, (ROWS, 2 * DH), 1) < DH
    zero = jnp.zeros((ROWS, 2 * DH), bf)

    def stacked(x):
        return jnp.concatenate([jnp.where(low, x, zero), jnp.where(low, zero, x)], axis=0)

    def beside(x):
        return jnp.concatenate([x[:ROWS], x[ROWS:]], axis=1)

    copies = []
    for pair in range(H // 2):
        at = slice(pair * 2 * DH, (pair + 1) * 2 * DH)
        rows[pair] = got[:, at].astype(f32)
        q, k, v, g = (
            jnp.concatenate(
                [rows[pair, pl.ds(2 * n + r, CB, stride=8), :] for r in range(2)], axis=0
            ).astype(bf)
            for n in range(4)
        )
        qs, ks, vs, gs = (stacked(x) for x in (q, k, v, g))
        logits = dot(qs, k, 1, 1) * COL_SCALE
        dprobs = dot(gs, v, 1, 1)
        e = jnp.exp(logits - jnp.max(logits, axis=-1, keepdims=True))
        probs = e / jnp.sum(e, axis=-1, keepdims=True)
        dl = probs * (dprobs - jnp.sum(probs * dprobs, axis=-1, keepdims=True)) * COL_SCALE
        pb = probs.astype(bf)
        db = dl.astype(bf)
        res = (
            dot(beside(pb), vs, 1, 0),
            dot(beside(db), ks, 1, 0),
            dot(db, qs, 0, 0),
            dot(pb, gs, 0, 0),
        )
        for n in range(4):
            for r in range(2):
                rows[pair, pl.ds(2 * n + r, CB, stride=8), :] = res[n][r * CB : (r + 1) * CB]
        made[pair] = rows[pair].astype(bf)
        copies.append(pltpu.make_async_copy(made.at[pair], out.at[:, at], sems.at[pair]))
        copies[-1].start()
    for copy in copies:
        copy.wait()


def column_finish_kernel(columns, col_out, grad_cq, grad_ck, grad_cv, rows):
    for pair in range(H // 2):
        at = slice(pair * 2 * DH, (pair + 1) * 2 * DH)
        rows[pair] = columns[:, at].astype(f32)
        for n, ref in enumerate((col_out, grad_cq, grad_ck, grad_cv)):
            for r in range(2):
                ref[r, :, at] = rows[pair, pl.ds(2 * n + r, CB, stride=8), :].astype(bf)


def finish_kernel(heads, col_out, update, grad_rq, grad_rk, grad_rv):
    for pair in range(H // 2):
        at = slice(pair * 2 * DH, (pair + 1) * 2 * DH)
        for n, ref in enumerate((update, grad_rq, grad_rk, grad_rv)):
            a, b = (
                jnp.concatenate([heads[h // HL * NC + c, n, h % HL] for c in range(NC)], axis=0)
                for h in (2 * pair, 2 * pair + 1)
            )
            for r in range(2):
                got = jnp.concatenate(
                    [a[:, r * DH : (r + 1) * DH], b[:, r * DH : (r + 1) * DH]], axis=1
                )
                if n == 0:
                    got = (got.astype(f32) + col_out[r, :, at].astype(f32)).astype(bf)
                ref[r, :, at] = got


def swap(array, axes):
    return lax.all_to_all(array, axes, 0, 0, tiled=True)


def on_device(row_q, row_k, row_v, col_q, col_k, col_v, cotangent):
    dev = sds((2, CB, H * DH), bf)
    flat = sds((CB * 8, H * DH), bf)
    room = pltpu.VMEM((H // 2, CB * 8, 2 * DH), f32)
    by_head = call(
        to_heads_kernel,
        sds((NHG * NC, 4, HL, HC, 2 * DH), bf),
        row_k,
        row_v,
        row_q,
        cotangent,
        scratch=[
            pltpu.VMEM((4, 2, CB, H * DH), bf),
            pltpu.VMEM((4, NHG * NC, HL, HC, 2 * DH), bf),
            pltpu.SemaphoreType.DMA((4,)),
            pltpu.SemaphoreType.DMA((4,)),
        ],
        inside="far",
    )
    mine = swap(by_head, NEAR)
    cols = call(by_column_kernel, flat, col_q, col_k, col_v, cotangent, scratch=[room])
    cols, mine = lax.optimization_barrier((cols, mine))
    first = lax.axis_index("core") == 0
    other = lax.ppermute(mine, "core", [(0, 1), (1, 0)])

    def spread(n):
        own, far = mine[:, n : n + 2], other[:, n : n + 2]
        both = jnp.stack([jnp.where(first, own, far), jnp.where(first, far, own)])
        return lax.all_gather(both, "x", axis=0)

    keys_values = spread(0)
    queries_grads = spread(2)
    mine = mine[:, 2:]

    cols = swap(cols, COLUMN)
    cols = call(
        column_kernel,
        flat,
        cols,
        scratch=[
            room,
            pltpu.VMEM((H // 2, CB * 8, 2 * DH), bf),
            pltpu.SemaphoreType.DMA((H // 2,)),
        ],
        out_inside="far",
        flops=10**9,
    )
    cols = swap(cols, COLUMN)

    parts = call(
        logits_kernel,
        sds((NRED, 6 * QR, COLS // 2), bf),
        mine,
        keys_values,
    )
    cols, parts = lax.optimization_barrier((cols, parts))
    parts = swap(parts, RED)
    rows = call(softmax_kernel, sds((NRED, 2 * QR, COLS), bf), parts)
    rows = swap(rows, RED)
    col_out, grad_cq, grad_ck, grad_cv = call(
        column_finish_kernel, [dev] * 4, cols, scratch=[room], inside=False
    )
    rows, queries_grads, col_out = lax.optimization_barrier((rows, queries_grads, col_out))
    probs, dlogits, by_key = call(
        assemble_kernel,
        [
            sds((HL * CB, COLS), bf),
            sds((HL * CB, COLS), bf),
            sds((NRES, HL * CB, 2 * CB), bf),
        ],
        rows,
    )
    by_query = swap(by_key, BLOCKS)
    back = call(
        row_grads_kernel,
        sds((NHG * NC, 4, HL, HC, 2 * DH), bf),
        probs,
        dlogits,
        by_query,
        keys_values,
        queries_grads,
    )
    back = swap(back, NEAR)
    update, grad_rq, grad_rk, grad_rv = call(
        finish_kernel, [dev] * 4, back, col_out, out_inside=False
    )
    return update, grad_rq, grad_rk, grad_rv, grad_cq, grad_ck, grad_cv


def solution(mesh):
    fine = Mesh(
        mesh.devices.reshape(4, 2, 4, 2, 2, 4), ("yhi", "ylo", "zhi", "core", "zlo", "x")
    )
    spec = P(DEP, RES, None)
    return jax.shard_map(
        on_device, mesh=fine, in_specs=(spec,) * 7, out_specs=(spec,) * 7, check_vma=False
    )
```

```python
import math

import jax
import jax.numpy as jnp
from jax import lax
from jax.experimental import pallas as pl
from jax.experimental.pallas import tpu as pltpu
from jax.sharding import Mesh, PartitionSpec as P

H = 12
DH = 64
ROWS = 128
COLS = 512
NEAR = ("ylo", "zlo", "core")
RED = ("zhi", "yhi")
DEP = ("yhi", "ylo", "zhi", "core")
COLUMN = ("zhi", "yhi", "ylo", "core")
RES = ("zlo", "x")
BLOCKS = ("core", "x")
NHG = 4
SEQS = ((0, 0), (0, 1), (1, 0), (1, 1))
HL = 3
NRED = 16
NRES = 8
NX = 4
NZ = 2
NC = 2
HC = 32
CB = 64
QR = HL * CB // NRED
ROW_SCALE = 1.0 / math.sqrt(DH) / math.sqrt(ROWS)
COL_SCALE = 1.0 / math.sqrt(DH)
HALVES = (slice(0, COLS // 2), slice(COLS // 2, COLS))
bf = jnp.bfloat16
f32 = jnp.float32


def call(body, out_shape, *args, scratch=(), inside=True, out_inside=None, flops=10**7):
    many = isinstance(out_shape, (list, tuple))
    outs = out_shape if many else [out_shape]
    nbytes = sum(math.prod(a.shape) * a.dtype.itemsize for a in list(args) + list(outs))
    specs = {
        True: pl.BlockSpec(memory_space=pltpu.VMEM),
        False: pl.BlockSpec(),
        "far": pl.BlockSpec(memory_space=pl.ANY),
    }
    spec, out_spec = specs[inside], specs[inside if out_inside is None else out_inside]
    return pl.pallas_call(
        body,
        out_shape=out_shape,
        in_specs=[spec] * len(args),
        out_specs=[out_spec] * len(outs) if many else out_spec,
        scratch_shapes=list(scratch),
        compiler_params=pltpu.CompilerParams(vmem_limit_bytes=(24 if inside is True else 56) * 2**20),
        cost_estimate=pl.CostEstimate(flops=flops, bytes_accessed=nbytes, transcendentals=0),
    )(*args)


def sds(shape, dtype):
    return jax.ShapeDtypeStruct(shape, dtype)


def dot(a, b, ca, cb):
    return lax.dot_general(a, b, (((ca,), (cb,)), ((), ())), preferred_element_type=f32)


def to_heads_kernel(*refs):
    arrays, (out, got, made, in_sems, out_sems) = refs[:4], refs[4:]
    reads = [
        pltpu.make_async_copy(ref, got.at[n], in_sems.at[n]) for n, ref in enumerate(arrays)
    ]
    for copy in reads:
        copy.start()
    writes = []
    for n, read in enumerate(reads):
        read.wait()
        for h in range(H):
            a = got[n, 0, :, h * DH : (h + 1) * DH]
            b = got[n, 1, :, h * DH : (h + 1) * DH]
            both = jnp.concatenate([a, b], axis=1)
            for c in range(NC):
                made[n, h // HL * NC + c, h % HL] = both[c * HC : (c + 1) * HC]
        writes.append(pltpu.make_async_copy(made.at[n], out.at[:, n], out_sems.at[n]))
        writes[-1].start()
    for copy in writes:
        copy.wait()


def block(ref, at, n, h):
    return jnp.concatenate(
        [
            jnp.concatenate([ref[(*at, (y * NZ + z) * NC + c, n, h)] for y, c in SEQS], axis=1)
            for z in range(NZ)
        ],
        axis=0,
    )


def gathered(refs, n, h):
    return jnp.concatenate([block(ref, (x,), n, h) for ref in refs for x in range(NX)], axis=0)


def place(slot):
    return (slot // NX + lax.axis_index("core")) % NC * NX + slot % NX


def logits_kernel(mine, near, far, out):
    logits, dprobs = [], []
    for h in range(HL):
        for res, n, which in ((logits, 0, 0), (dprobs, 1, 1)):
            res.append(dot(block(mine, (), n, h), gathered((near, far), which, h), 1, 1))
    logits = jnp.concatenate(logits, axis=0)
    dprobs = jnp.concatenate(dprobs, axis=0)
    dprobs = dprobs - jnp.mean(dprobs, axis=-1, keepdims=True)
    high = logits.astype(bf).astype(f32)
    rest = logits - high
    for m in range(NRED):
        at = slice(m * QR, (m + 1) * QR)
        out[m] = jnp.concatenate(
            [a[at, half] for a in (high, rest, dprobs) for half in HALVES], axis=0
        ).astype(bf)


def softmax_kernel(parts, out):
    total = parts[0].astype(f32)
    for m in range(1, NRED):
        total = total + parts[m].astype(f32)
    high, rest, dprobs = (
        jnp.concatenate([total[n * QR : (n + 1) * QR], total[(n + 1) * QR : (n + 2) * QR]], axis=1)
        for n in (0, 2, 4)
    )
    logits = (high + rest) * ROW_SCALE
    e = jnp.exp(logits - jnp.max(logits, axis=-1, keepdims=True))
    probs = e / jnp.sum(e, axis=-1, keepdims=True)
    dl = probs * (dprobs - jnp.sum(probs * dprobs, axis=-1, keepdims=True)) * ROW_SCALE
    both = jnp.concatenate([probs, dl], axis=0).astype(bf)
    for m in range(NRED):
        out[m] = both


def assemble_kernel(rows, probs, dlogits, by_key):
    parts = [rows[m].astype(f32) for m in range(NRED)]
    p = jnp.concatenate([a[:QR] for a in parts], axis=0).astype(bf)
    d = jnp.concatenate([a[QR:] for a in parts], axis=0).astype(bf)
    probs[...] = p
    dlogits[...] = d
    for r in range(NRES):
        by_key[place(r)] = jnp.concatenate(
            [p[:, r * CB : (r + 1) * CB], d[:, r * CB : (r + 1) * CB]], axis=1
        )


def row_grads_kernel(probs, dlogits, by_query, near_kv, far_kv, near_qg, far_qg, out):

    def put(n, h, res):
        for z in range(NZ):
            for s, (y, c) in enumerate(SEQS):
                out[(y * NZ + z) * NC + c, n, h] = res[
                    z * HC : (z + 1) * HC, s * 2 * DH : (s + 1) * 2 * DH
                ].astype(bf)

    for h in range(HL):
        at = slice(h * CB, (h + 1) * CB)
        put(0, h, dot(probs[at, :], gathered((near_kv, far_kv), 1, h), 1, 0))
        put(1, h, dot(dlogits[at, :], gathered((near_kv, far_kv), 0, h), 1, 0))
        lhs = jnp.concatenate([by_query[place(r), at, :] for r in range(NRES)], axis=0)
        put(2, h, dot(lhs, gathered((near_qg, far_qg), 0, h), 0, 0)[CB:])
        put(3, h, dot(lhs, gathered((near_qg, far_qg), 1, h), 0, 0)[:CB])


def by_column_kernel(query, keys, values, grads, out, rows):
    for pair in range(H // 2):
        at = slice(pair * 2 * DH, (pair + 1) * 2 * DH)
        for n, ref in enumerate((query, keys, values, grads)):
            for r in range(2):
                rows[pair, pl.ds(2 * n + r, CB, stride=8), :] = ref[r, :, at].astype(f32)
        out[:, at] = rows[pair].astype(bf)


def column_kernel(got, out, rows, made, sems):
    low = lax.broadcasted_iota(jnp.int32, (ROWS, 2 * DH), 1) < DH
    zero = jnp.zeros((ROWS, 2 * DH), bf)

    def stacked(x):
        return jnp.concatenate([jnp.where(low, x, zero), jnp.where(low, zero, x)], axis=0)

    def beside(x):
        return jnp.concatenate([x[:ROWS], x[ROWS:]], axis=1)

    copies = []
    for pair in range(H // 2):
        at = slice(pair * 2 * DH, (pair + 1) * 2 * DH)
        rows[pair] = got[:, at].astype(f32)
        q, k, v, g = (
            jnp.concatenate(
                [rows[pair, pl.ds(2 * n + r, CB, stride=8), :] for r in range(2)], axis=0
            ).astype(bf)
            for n in range(4)
        )
        qs, ks, vs, gs = (stacked(x) for x in (q, k, v, g))
        logits = dot(qs, k, 1, 1) * COL_SCALE
        dprobs = dot(gs, v, 1, 1)
        e = jnp.exp(logits - jnp.max(logits, axis=-1, keepdims=True))
        probs = e / jnp.sum(e, axis=-1, keepdims=True)
        dl = probs * (dprobs - jnp.sum(probs * dprobs, axis=-1, keepdims=True)) * COL_SCALE
        pb = probs.astype(bf)
        db = dl.astype(bf)
        res = (
            dot(beside(pb), vs, 1, 0),
            dot(beside(db), ks, 1, 0),
            dot(db, qs, 0, 0),
            dot(pb, gs, 0, 0),
        )
        for n in range(4):
            for r in range(2):
                rows[pair, pl.ds(2 * n + r, CB, stride=8), :] = res[n][r * CB : (r + 1) * CB]
        made[pair] = rows[pair].astype(bf)
        copies.append(pltpu.make_async_copy(made.at[pair], out.at[:, at], sems.at[pair]))
        copies[-1].start()
    for copy in copies:
        copy.wait()


def column_finish_kernel(columns, col_out, grad_cq, grad_ck, grad_cv, rows):
    for pair in range(H // 2):
        at = slice(pair * 2 * DH, (pair + 1) * 2 * DH)
        rows[pair] = columns[:, at].astype(f32)
        for n, ref in enumerate((col_out, grad_cq, grad_ck, grad_cv)):
            for r in range(2):
                ref[r, :, at] = rows[pair, pl.ds(2 * n + r, CB, stride=8), :].astype(bf)


def finish_kernel(heads, col_out, update, grad_rq, grad_rk, grad_rv):
    for pair in range(H // 2):
        at = slice(pair * 2 * DH, (pair + 1) * 2 * DH)
        for n, ref in enumerate((update, grad_rq, grad_rk, grad_rv)):
            a, b = (
                jnp.concatenate([heads[h // HL * NC + c, n, h % HL] for c in range(NC)], axis=0)
                for h in (2 * pair, 2 * pair + 1)
            )
            for r in range(2):
                got = jnp.concatenate(
                    [a[:, r * DH : (r + 1) * DH], b[:, r * DH : (r + 1) * DH]], axis=1
                )
                if n == 0:
                    got = (got.astype(f32) + col_out[r, :, at].astype(f32)).astype(bf)
                ref[r, :, at] = got


def swap(array, axes):
    return lax.all_to_all(array, axes, 0, 0, tiled=True)


def on_device(row_q, row_k, row_v, col_q, col_k, col_v, cotangent):
    dev = sds((2, CB, H * DH), bf)
    flat = sds((CB * 8, H * DH), bf)
    room = pltpu.VMEM((H // 2, CB * 8, 2 * DH), f32)
    by_head = call(
        to_heads_kernel,
        sds((NHG * NC, 4, HL, HC, 2 * DH), bf),
        row_k,
        row_v,
        row_q,
        cotangent,
        scratch=[
            pltpu.VMEM((4, 2, CB, H * DH), bf),
            pltpu.VMEM((4, NHG * NC, HL, HC, 2 * DH), bf),
            pltpu.SemaphoreType.DMA((4,)),
            pltpu.SemaphoreType.DMA((4,)),
        ],
        inside="far",
    )
    mine = swap(by_head, NEAR)
    cols = call(by_column_kernel, flat, col_q, col_k, col_v, cotangent, scratch=[room])
    cols, mine = lax.optimization_barrier((cols, mine))
    near_kv = lax.all_gather(mine[:, :2], "x", axis=0)
    other = lax.ppermute(mine, "core", [(0, 1), (1, 0)])

    cols = swap(cols, COLUMN)
    cols, other, mine = lax.optimization_barrier((cols, other, mine))
    far_kv = lax.all_gather(other[:, :2], "x", axis=0)
    cols = call(
        column_kernel,
        flat,
        cols,
        scratch=[
            room,
            pltpu.VMEM((H // 2, CB * 8, 2 * DH), bf),
            pltpu.SemaphoreType.DMA((H // 2,)),
        ],
        out_inside="far",
        flops=10**9,
    )
    cols, other, mine = lax.optimization_barrier((cols, other[:, 2:], mine[:, 2:]))
    near_qg = lax.all_gather(mine, "x", axis=0)
    far_qg = lax.all_gather(other, "x", axis=0)
    cols = swap(cols, COLUMN)

    parts = call(
        logits_kernel,
        sds((NRED, 6 * QR, COLS // 2), bf),
        mine,
        near_kv,
        far_kv,
    )
    cols, parts = lax.optimization_barrier((cols, parts))
    parts = swap(parts, RED)
    rows = call(softmax_kernel, sds((NRED, 2 * QR, COLS), bf), parts)
    rows = swap(rows, RED)
    col_out, grad_cq, grad_ck, grad_cv = call(
        column_finish_kernel, [dev] * 4, cols, scratch=[room], inside=False
    )
    rows, near_qg, far_qg, col_out = lax.optimization_barrier(
        (rows, near_qg, far_qg, col_out)
    )
    probs, dlogits, by_key = call(
        assemble_kernel,
        [
            sds((HL * CB, COLS), bf),
            sds((HL * CB, COLS), bf),
            sds((NRES, HL * CB, 2 * CB), bf),
        ],
        rows,
    )
    by_query = swap(by_key, BLOCKS)
    back = call(
        row_grads_kernel,
        sds((NHG * NC, 4, HL, HC, 2 * DH), bf),
        probs,
        dlogits,
        by_query,
        near_kv,
        far_kv,
        near_qg,
        far_qg,
    )
    back = swap(back, NEAR)
    update, grad_rq, grad_rk, grad_rv = call(
        finish_kernel, [dev] * 4, back, col_out, out_inside=False
    )
    return update, grad_rq, grad_rk, grad_rv, grad_cq, grad_ck, grad_cv


def solution(mesh):
    fine = Mesh(
        mesh.devices.reshape(4, 2, 4, 2, 2, 4), ("yhi", "ylo", "zhi", "core", "zlo", "x")
    )
    spec = P(DEP, RES, None)
    return jax.shard_map(
        on_device, mesh=fine, in_specs=(spec,) * 7, out_specs=(spec,) * 7, check_vma=False
    )
```
